32 devices in a mesh: grp: 2 (over x), dp: 4 (over z), mp: 4 (over y, core).
Axes of the slice: x: 2, y: 2, z: 4, core: 2. Of those that a mesh axis runs over, the one named last changes fastest.
Arguments:
- captured: bfloat16 [3, 256, 8192], P(None, 'mp', ('grp', 'dp')), may hold values from -9 to 9
- unite_weight: bfloat16 [3, 8192, 8192], P(None, ('grp', 'dp'), 'mp'), may hold values from -0.0390625 to 0.0390625
- heads: bfloat16 [2, 16000, 8192], P('grp', 'dp', 'mp'), may hold values from -10 to 10, as said below
- final_hidden: bfloat16 [256, 8192], P('dp', 'mp'), may hold values from -9 to 9
- target_gain: float32 [8192], P('mp'), may hold values from 0.1 to 1.9
- draft_gain: float32 [8192], P('mp'), may hold values from 0.1 to 1.9
- lengths: int32 [4], replicated, may hold values from 32 to 64
Outputs:
- grad_terms: bfloat16 [2, 16000, 8192], P('grp', 'dp', 'mp')
- token_loss: float32 [256], P('mp')
The draws below stay inside these ranges and needn't reach their ends.
Inputs may be any that keep to these rules, and one draw needn't show every extreme that they name: `heads`: each row of a head has its own scale.
All inputs are finite; a program needn't handle non-finite values.
Results may differ from the reference program's by a relative error of at most 0.0051.
Values may be sent and summed in bfloat16 or wider, within the bound.
A program may use at most 128 MiB of HBM per device.

```python
import math
import jax
import jax.numpy as jnp
from jax import lax

D = 8192
DV = 16000
LAYERS = 3
TOK_DEV = 64
SLABS = 4
TOKENS = 256


def draw_heads(key, part):
    normal_key, scale_key = jax.random.split(jax.random.fold_in(key, 11), 2)
    normal_base = jnp.clip(jax.random.normal(normal_key, (2, DV, D), jnp.float32), -6.0, 6.0) / math.sqrt(D)
    row_scale = jnp.exp(jax.random.uniform(scale_key, (2, DV, 1), jnp.float32, math.log(0.2), math.log(2.5)))
    return jnp.clip(normal_base * row_scale, -10.0, 10.0).astype(jnp.bfloat16)


def common_direction(key, amp_low, amp_high):
    direction_key, amplitude_key = jax.random.split(jax.random.fold_in(key, 29), 2)
    direction = jnp.clip(jax.random.normal(direction_key, (D,), jnp.float32), -3.0, 3.0)
    amplitude = jax.random.uniform(amplitude_key, (TOKENS,), jnp.float32, amp_low, amp_high)
    return (direction, amplitude)


def draw_final_hidden(key, part):
    noise_key = jax.random.fold_in(key, 31)
    direction, amplitude = common_direction(key, 0.4, 1.2)
    noise = jnp.clip(jax.random.normal(noise_key, (TOKENS, D), jnp.float32), -6.0, 6.0)
    values = noise + 0.8 * amplitude[:, None] * direction[None, :]
    return values.astype(jnp.bfloat16)


def draw_captured(key, part):
    noise_key = jax.random.fold_in(key, 37)
    direction, amplitude = common_direction(key, 0.4, 1.2)
    noise = jnp.clip(jax.random.normal(noise_key, (LAYERS, TOKENS, D), jnp.float32), -6.0, 6.0)
    values = noise + 0.8 * amplitude[None, :, None] * direction[None, None, :]
    return values.astype(jnp.bfloat16)


def with_ends(result, rng, smallest, largest):
    place = [jax.random.randint(jax.random.fold_in(rng, axis), (), 0, length) for axis, length in enumerate(result.shape)]
    main_axis = result.shape.index(max(result.shape))
    beside = place[:main_axis] + [(place[main_axis] + 1) % result.shape[main_axis]] + place[main_axis + 1:]
    return result.at[tuple(place)].set(smallest).at[tuple(beside)].set(largest)


def level_of(rng, shape, cuts, low, high):
    def one(axis_at, blocks):
        draws = jax.random.uniform(jax.random.fold_in(jax.random.fold_in(rng, 6), axis_at), (blocks,), jnp.float32, low / len(cuts), high / len(cuts))
        return jnp.repeat(jnp.exp(draws), shape[axis_at] // blocks).reshape((-1,) + (1,) * (len(shape) - axis_at - 1))

    loudness = one(*cuts[0])
    for cut in cuts[1:]:
        loudness = loudness * one(*cut)
    return loudness


def centred(rng, dims, width, reach, cuts=(), held_as=jnp.bfloat16):
    result = width * jax.random.normal(rng, dims, jnp.float32)
    if cuts:
        result = result * level_of(rng, dims, cuts, -0.22, 0.18)
    return jnp.clip(result, -reach, reach).astype(held_as)


def setup_inputs(seed: int = 0) -> dict:
    key_of = jax.random.split(jax.random.key(seed), 8)
    captured = draw_captured(jax.random.fold_in(key_of[7], 71), 0)
    unite_weight = centred(key_of[1], (LAYERS, D, D), (LAYERS * D) ** -0.5, 0.0390625, ((1, 8), (2, 4)))
    heads = draw_heads(jax.random.fold_in(key_of[7], 71), 0)
    final_hidden = draw_final_hidden(jax.random.fold_in(key_of[7], 71), 0)
    target_gain = jnp.clip(1.0 + 0.18 * jax.random.normal(key_of[4], (D,), jnp.float32), 0.1, 1.9)
    draft_gain = jnp.clip(1.0 + 0.18 * jax.random.normal(key_of[5], (D,), jnp.float32), 0.1, 1.9)
    lengths = with_ends(jax.random.randint(key_of[6], (SLABS,), TOK_DEV // 2, TOK_DEV + 1), jax.random.fold_in(key_of[6], 1), TOK_DEV // 2, TOK_DEV).astype(jnp.int32)
    return {"captured": captured, "unite_weight": unite_weight, "heads": heads, "final_hidden": final_hidden, "target_gain": target_gain, "draft_gain": draft_gain, "lengths": lengths}


EPSILON = 1e-05

def normalize(row_values, gain_vector):
    values = row_values.astype(jnp.float32)
    inverse_rms = lax.rsqrt(lax.optimization_barrier(jnp.mean(values * values, axis=1, keepdims=True)) + EPSILON)
    return (values * inverse_rms * gain_vector[None, :]).astype(jnp.bfloat16)

def united_features(captured, unite_weight):
    summed = jnp.dot(captured[0], unite_weight[0], preferred_element_type=jnp.float32)
    for layer_index in range(1, LAYERS):
        summed = summed + jnp.dot(captured[layer_index], unite_weight[layer_index], preferred_element_type=jnp.float32)
    return summed

def vocab_logits(row_values, head_rows):
    return jnp.dot(row_values, head_rows.T, preferred_element_type=jnp.float32)

def softmax_parts(logits):
    row_max = lax.optimization_barrier(jnp.max(logits, axis=1, keepdims=True))
    shifted = logits - row_max
    row_total = lax.optimization_barrier(jnp.sum(jnp.exp(shifted), axis=1, keepdims=True))
    return (jnp.exp(shifted) / row_total, shifted - jnp.log(row_total))

def reference(captured, unite_weight, heads, final_hidden, target_gain, draft_gain, lengths):
    united = united_features(captured, unite_weight)
    draft_rows = normalize(united, draft_gain)
    target_rows = normalize(final_hidden, target_gain)
    target_probs, unused_logs = softmax_parts(vocab_logits(target_rows, heads[0]))
    draft_probs, draft_logs = softmax_parts(vocab_logits(draft_rows, heads[1]))
    token_index = jnp.arange(TOKENS, dtype=jnp.int32)
    slab_index = token_index // TOK_DEV
    position = token_index - slab_index * TOK_DEV
    valid_mask = (position < lengths[slab_index]).astype(jnp.float32)
    valid_total = jnp.sum(lengths).astype(jnp.float32)
    token_loss = -valid_mask * lax.optimization_barrier(jnp.sum(target_probs * draft_logs, axis=1))
    weights = (valid_mask / valid_total)[:, None]
    target_weighted = (target_probs * weights).astype(jnp.bfloat16)
    delta_weighted = ((draft_probs - target_probs) * weights).astype(jnp.bfloat16)
    target_term = jnp.dot(target_weighted.T, draft_rows, preferred_element_type=jnp.float32)
    delta_term = jnp.dot(delta_weighted.T, draft_rows, preferred_element_type=jnp.float32)
    grad_terms = jnp.stack([(-target_term).astype(jnp.bfloat16), delta_term.astype(jnp.bfloat16)])
    return (grad_terms, token_loss)
```

```python
import functools

import jax
import jax.numpy as jnp
from jax import lax
from jax.experimental import pallas as pl
from jax.experimental.pallas import tpu as pltpu
from jax.sharding import PartitionSpec as P

EPSILON = 1e-05
PARTIAL = jnp.bfloat16
MESH = pl.DeviceIdType.MESH


def whole_axis(axis):
    return lambda: (lax.axis_size(axis), lax.axis_index(axis), lambda p: {axis: p})


def both_axes():
    outer, inner = lax.axis_size("grp"), lax.axis_size("dp")
    me = lax.axis_index("grp") * inner + lax.axis_index("dp")
    return (outer * inner, me, lambda p: {"grp": lax.div(p, inner), "dp": lax.rem(p, inner)})


def pair():
    index = lax.axis_index("mp")
    return (2, lax.rem(index, 2), lambda p: {"mp": lax.div(index, 2) * 2 + p})


def across():
    index = lax.axis_index("mp")
    count = lax.axis_size("mp") // 2
    return (count, lax.div(index, 2), lambda p: {"mp": p * 2 + lax.rem(index, 2)})


def rows_at(ref, dim, index, size):
    window = pl.ds(pl.multiple_of(index * size, size), size)
    return ref.at[(slice(None),) * dim + (window,)]


def exchange_body(items, *refs):
    count = len(items)
    ins, outs = refs[:count], refs[count : 2 * count]
    local_sem, send_sem, recv_sem = refs[2 * count :]
    groups = [item[0]() for item in items]
    barrier = pltpu.get_barrier_semaphore()
    total = 0
    for n, me, place in groups:
        for k in range(1, n):
            pl.semaphore_signal(
                barrier, inc=1, device_id=place(lax.rem(me + k, n)), device_id_type=MESH
            )
        total += n - 1
    pl.semaphore_wait(barrier, total)
    copies = []
    slot = 0
    for number, ((_, kind, dim), (n, me, place)) in enumerate(zip(items, groups)):
        source, target = ins[number], outs[number]
        size = target.shape[dim] // n
        landing = rows_at(target, dim, me, size)
        for k in range(1, n):
            peer = lax.rem(me + k, n)
            sent = source if kind == "gather" else rows_at(source, dim, peer, size)
            copy = pltpu.make_async_remote_copy(
                src_ref=sent,
                dst_ref=landing,
                send_sem=send_sem.at[slot],
                recv_sem=recv_sem.at[slot],
                device_id=place(peer),
                device_id_type=MESH,
            )
            copy.start()
            copies.append(copy)
            slot += 1
        kept = source if kind == "gather" else rows_at(source, dim, me, size)
        own = pltpu.make_async_copy(kept, landing, local_sem.at[number])
        own.start()
        copies.append(own)
    for copy in copies:
        copy.wait()


def exchange(number, arrays, items):
    shapes = []
    slots = 0
    for array, (group, kind, dim) in zip(arrays, items):
        n = group()[0]
        slots += n - 1
        shape = list(array.shape)
        if kind == "gather":
            shape[dim] *= n
        shapes.append(jax.ShapeDtypeStruct(tuple(shape), array.dtype))
    return pl.pallas_call(
        functools.partial(exchange_body, items),
        out_shape=shapes,
        in_specs=[pl.BlockSpec(memory_space=pl.ANY)] * len(arrays),
        out_specs=[pl.BlockSpec(memory_space=pl.ANY)] * len(arrays),
        scratch_shapes=[
            pltpu.SemaphoreType.DMA((len(arrays),)),
            pltpu.SemaphoreType.DMA((slots,)),
            pltpu.SemaphoreType.DMA((slots,)),
        ],
        compiler_params=pltpu.CompilerParams(collective_id=number, has_side_effects=True),
    )(*arrays)


def as_tile(parts):
    flat = jnp.concatenate([part.reshape(-1) for part in parts])
    padded = -(-flat.shape[0] // 1024) * 1024
    return jnp.pad(flat, (0, padded - flat.shape[0])).reshape(1, -1, 128)


def per_device(captured, unite_weight, heads, final_hidden, target_gain, draft_gain, lengths):
    mp_size = lax.axis_size("mp")
    dp_size = lax.axis_size("dp")
    grp_size = lax.axis_size("grp")
    model_width = final_hidden.shape[1] * mp_size
    slab_length = final_hidden.shape[0]
    is_target = lax.axis_index("grp") == 0
    head_rows = heads[0]
    segment, last = exchange(
        1,
        (captured, final_hidden),
        ((whole_axis("mp"), "gather", 1), (whole_axis("dp"), "gather", 0)),
    )
    tokens = last.shape[0]
    running = jnp.dot(segment[0], unite_weight[0], preferred_element_type=jnp.float32)
    for layer_index in range(1, segment.shape[0]):
        running = running + jnp.dot(
            segment[layer_index], unite_weight[layer_index], preferred_element_type=jnp.float32
        )
    members = grp_size * dp_size
    (arrived,) = exchange(2, (running.astype(PARTIAL),), ((both_axes, "swap", 0),))
    share = tokens // members
    arrived = arrived.reshape(members, share, -1)
    united = jnp.sum(arrived.astype(jnp.float32), axis=0)
    last_values = last.astype(jnp.float32)
    (squares,) = exchange(
        3,
        (as_tile([jnp.sum(united * united, axis=1), jnp.sum(last_values * last_values, axis=1)]),),
        ((whole_axis("mp"), "gather", 0),),
    )
    squares = jnp.sum(squares, axis=0).reshape(-1)
    draft_scale = lax.rsqrt(squares[:share] / model_width + EPSILON)
    target_scale = lax.rsqrt(squares[share : share + tokens] / model_width + EPSILON)
    draft_part = (united * draft_scale[:, None] * draft_gain[None, :]).astype(jnp.bfloat16)
    target_rows = (last_values * target_scale[:, None] * target_gain[None, :]).astype(jnp.bfloat16)
    (draft_rows,) = exchange(4, (draft_part,), ((both_axes, "gather", 0),))
    own_rows = jnp.where(is_target, target_rows, draft_rows)
    row_share = tokens // mp_size
    partial_logits = jnp.einsum(
        "td,vd->tv", own_rows, head_rows, preferred_element_type=jnp.float32
    )
    vocab = partial_logits.shape[1]
    by_core = partial_logits.reshape(mp_size // 2, 2, row_share, vocab)
    (by_core,) = exchange(5, (by_core,), ((pair, "swap", 1),))
    by_chip = by_core[:, 0] + by_core[:, 1]
    (by_chip,) = exchange(6, (by_chip,), ((across, "swap", 0),))
    logits = jnp.sum(by_chip, axis=0)
    local_max = jnp.max(logits, axis=1)
    shifted = logits - local_max[:, None]
    raised = jnp.exp(shifted)
    local_total = jnp.sum(raised, axis=1)
    incoming = lax.ppermute(raised.astype(jnp.bfloat16), "grp", [(0, 1)]).astype(jnp.float32)
    crossed = jnp.sum(incoming * shifted, axis=1)
    incoming_total = jnp.sum(incoming, axis=1)
    (stats,) = exchange(
        7,
        (as_tile([local_max, local_total, crossed, incoming_total]),),
        ((both_axes, "gather", 0),),
    )
    stats = stats.reshape(grp_size, dp_size, -1)[:, :, : 4 * row_share]
    stats = stats.reshape(grp_size, dp_size, 4, row_share)
    maxima, totals = stats[:, :, 0], stats[:, :, 1]
    row_max = jnp.max(maxima, axis=1)
    lift = jnp.exp(maxima - row_max[:, None])
    row_total = jnp.sum(lift * totals, axis=1)
    log_total = jnp.log(row_total)
    gap = maxima[1] - row_max[1][None] - log_total[1][None]
    cross_term = jnp.sum(lift[0] * (stats[1, :, 2] + gap * stats[1, :, 3]), axis=0) / row_total[0]

    token_index = lax.axis_index("mp") * row_share + lax.iota(jnp.int32, row_share)
    slab_index = token_index // slab_length
    position = token_index - slab_index * slab_length
    matches = slab_index[:, None] == lax.iota(jnp.int32, lengths.shape[0])[None, :]
    valid_len = jnp.sum(jnp.where(matches, lengths[None, :], 0), axis=1)
    valid_mask = (position < valid_len).astype(jnp.float32)
    valid_total = jnp.sum(lengths).astype(jnp.float32)
    token_loss = -valid_mask * cross_term
    here = lax.axis_index("dp")
    own_lift = lax.dynamic_index_in_dim(lift, here, axis=1, keepdims=False)
    factor = own_lift / row_total * (valid_mask / valid_total)[None]
    own_factor = jnp.where(is_target, factor[0], factor[1])
    other_factor = jnp.where(is_target, jnp.zeros_like(factor[0]), factor[0])
    weighted = (raised * own_factor[:, None] - incoming * other_factor[:, None]).astype(jnp.bfloat16)
    (all_weighted,) = exchange(8, (weighted,), ((whole_axis("mp"), "gather", 0),))
    summed = jnp.einsum(
        "tv,td->vd", all_weighted, draft_rows, preferred_element_type=jnp.float32
    )
    sign_factor = jnp.where(is_target, -1.0, 1.0).astype(jnp.float32)
    grad_terms = (sign_factor * summed).astype(jnp.bfloat16)[None]
    return (grad_terms, token_loss)


def solution(mesh):
    in_specs = (
        P(None, "mp", ("grp", "dp")),
        P(None, ("grp", "dp"), "mp"),
        P("grp", "dp", "mp"),
        P("dp", "mp"),
        P("mp"),
        P("mp"),
        P(),
    )
    out_specs = (P("grp", "dp", "mp"), P("mp"))
    return jax.shard_map(
        per_device, mesh=mesh, in_specs=in_specs, out_specs=out_specs, check_vma=False
    )
```

```python
import functools

import jax
import jax.numpy as jnp
from jax import lax
from jax.experimental import pallas as pl
from jax.experimental.pallas import tpu as pltpu
from jax.sharding import PartitionSpec as P

EPSILON = 1e-05
PARTIAL = jnp.bfloat16
MESH = pl.DeviceIdType.MESH


def whole_axis(axis):
    return lambda: (lax.axis_size(axis), lax.axis_index(axis), lambda p: {axis: p})


def both_axes():
    outer, inner = lax.axis_size("grp"), lax.axis_size("dp")
    me = lax.axis_index("grp") * inner + lax.axis_index("dp")
    return (outer * inner, me, lambda p: {"grp": lax.div(p, inner), "dp": lax.rem(p, inner)})


def pair():
    index = lax.axis_index("mp")
    return (2, lax.rem(index, 2), lambda p: {"mp": lax.div(index, 2) * 2 + p})


def across():
    index = lax.axis_index("mp")
    count = lax.axis_size("mp") // 2
    return (count, lax.div(index, 2), lambda p: {"mp": p * 2 + lax.rem(index, 2)})


def window(ref, dim, index, size):
    start = index * size if isinstance(index, int) else pl.multiple_of(index * size, size)
    return ref.at[(slice(None),) * dim + (pl.ds(start, size),)]


def exchange_body(items, *refs):
    count = len(items)
    ins, outs = refs[:count], refs[count : 2 * count]
    local_sem, send_sem, recv_sem = refs[2 * count :]
    groups = [item[0]() for item in items]
    barrier = pltpu.get_barrier_semaphore()
    total = 0
    for n, me, place in groups:
        for k in range(1, n):
            pl.semaphore_signal(
                barrier, inc=1, device_id=place(lax.rem(me + k, n)), device_id_type=MESH
            )
        total += n - 1
    pl.semaphore_wait(barrier, total)
    copies = []
    slot = 0
    for number, ((_, kind, dim, cut, pieces), (n, me, place)) in enumerate(zip(items, groups)):
        source, target = ins[number], outs[number]
        step = source.shape[cut] // pieces
        for k in range(1, n):
            peer = lax.rem(me + k, n)
            if kind == "gather":
                sent, landing = source, window(target, dim, me, source.shape[dim])
            else:
                size = source.shape[dim] // n
                sent, landing = window(source, dim, peer, size), window(target, dim, k - 1, size)
            for piece in range(pieces):
                copy = pltpu.make_async_remote_copy(
                    src_ref=sent if pieces == 1 else window(sent, cut, piece, step),
                    dst_ref=landing if pieces == 1 else window(landing, cut, piece, step),
                    send_sem=send_sem.at[slot],
                    recv_sem=recv_sem.at[slot],
                    device_id=place(peer),
                    device_id_type=MESH,
                )
                copy.start()
                copies.append(copy)
                slot += 1
        if kind == "gather":
            own = pltpu.make_async_copy(
                source, window(target, dim, me, source.shape[dim]), local_sem.at[number]
            )
            own.start()
            copies.append(own)
    for copy in copies:
        copy.wait()


def exchange(number, arrays, items):
    shapes = []
    slots = 0
    for array, (group, kind, dim, cut, pieces) in zip(arrays, items):
        n = group()[0]
        slots += (n - 1) * pieces
        shape = list(array.shape)
        shape[dim] = shape[dim] * n if kind == "gather" else shape[dim] // n * (n - 1)
        shapes.append(jax.ShapeDtypeStruct(tuple(shape), array.dtype))
    return pl.pallas_call(
        functools.partial(exchange_body, items),
        out_shape=shapes,
        in_specs=[pl.BlockSpec(memory_space=pl.ANY)] * len(arrays),
        out_specs=[pl.BlockSpec(memory_space=pl.ANY)] * len(arrays),
        scratch_shapes=[
            pltpu.SemaphoreType.DMA((len(arrays),)),
            pltpu.SemaphoreType.DMA((slots,)),
            pltpu.SemaphoreType.DMA((slots,)),
        ],
        compiler_params=pltpu.CompilerParams(collective_id=number, has_side_effects=True),
    )(*arrays)


def summed_over(number, parts, group, pieces):
    (arrived,) = exchange(number, (parts,), ((group, "swap", 0, 1, pieces),))
    own = lax.dynamic_index_in_dim(parts, group()[1], axis=0, keepdims=False)
    total = own.astype(jnp.float32)
    for k in range(arrived.shape[0]):
        total = total + arrived[k].astype(jnp.float32)
    return total


def as_tile(parts):
    flat = jnp.concatenate([part.reshape(-1) for part in parts])
    padded = -(-flat.shape[0] // 1024) * 1024
    return jnp.pad(flat, (0, padded - flat.shape[0])).reshape(1, -1, 128)


def per_device(captured, unite_weight, heads, final_hidden, target_gain, draft_gain, lengths):
    mp_size = lax.axis_size("mp")
    dp_size = lax.axis_size("dp")
    grp_size = lax.axis_size("grp")
    model_width = final_hidden.shape[1] * mp_size
    slab_length = final_hidden.shape[0]
    is_target = lax.axis_index("grp") == 0
    head_rows = heads[0]
    last = lax.all_gather(final_hidden, "dp", axis=0, tiled=True)
    layers = captured.shape[0]
    (segment,) = exchange(1, (captured,), ((whole_axis("mp"), "gather", 1, 0, layers),))
    tokens = last.shape[0]
    running = jnp.dot(segment[0], unite_weight[0], preferred_element_type=jnp.float32)
    for layer_index in range(1, segment.shape[0]):
        running = running + jnp.dot(
            segment[layer_index], unite_weight[layer_index], preferred_element_type=jnp.float32
        )
    members = grp_size * dp_size
    share = tokens // members
    united = summed_over(2, running.astype(PARTIAL).reshape(members, share, -1), both_axes, 1)
    last_values = last.astype(jnp.float32)
    (squares,) = exchange(
        3,
        (as_tile([jnp.sum(united * united, axis=1), jnp.sum(last_values * last_values, axis=1)]),),
        ((whole_axis("mp"), "gather", 0, 1, 1),),
    )
    squares = jnp.sum(squares, axis=0).reshape(-1)
    draft_scale = lax.rsqrt(squares[:share] / model_width + EPSILON)
    target_scale = lax.rsqrt(squares[share : share + tokens] / model_width + EPSILON)
    draft_part = (united * draft_scale[:, None] * draft_gain[None, :]).astype(jnp.bfloat16)
    target_rows = (last_values * target_scale[:, None] * target_gain[None, :]).astype(jnp.bfloat16)
    (draft_rows,) = exchange(4, (draft_part,), ((both_axes, "gather", 0, 1, 1),))
    own_rows = jnp.where(is_target, target_rows, draft_rows)
    row_share = tokens // mp_size
    partial_logits = jnp.einsum(
        "td,vd->tv", own_rows, head_rows, preferred_element_type=jnp.float32
    )
    vocab = partial_logits.shape[1]
    width = -(-vocab // 128) * 128
    partial_logits = jnp.pad(partial_logits, ((0, 0), (0, width - vocab)))
    by_core = partial_logits.reshape(mp_size // 2, 2, row_share, width)
    pieces = row_share // 8
    (swapped,) = exchange(5, (by_core,), ((pair, "swap", 1, 2, pieces),))
    by_chip = swapped[:, 0] + lax.dynamic_index_in_dim(by_core, pair()[1], axis=1, keepdims=False)
    logits = summed_over(6, by_chip, across, pieces)[:, :vocab]
    local_max = jnp.max(logits, axis=1)
    shifted = logits - local_max[:, None]
    raised = jnp.exp(shifted)
    local_total = jnp.sum(raised, axis=1)
    incoming = lax.ppermute(raised.astype(jnp.bfloat16), "grp", [(0, 1)]).astype(jnp.float32)
    crossed = jnp.sum(incoming * shifted, axis=1)
    incoming_total = jnp.sum(incoming, axis=1)
    (stats,) = exchange(
        7,
        (as_tile([local_max, local_total, crossed, incoming_total]),),
        ((both_axes, "gather", 0, 1, 1),),
    )
    stats = stats.reshape(grp_size, dp_size, -1)[:, :, : 4 * row_share]
    stats = stats.reshape(grp_size, dp_size, 4, row_share)
    maxima, totals = stats[:, :, 0], stats[:, :, 1]
    row_max = jnp.max(maxima, axis=1)
    lift = jnp.exp(maxima - row_max[:, None])
    row_total = jnp.sum(lift * totals, axis=1)
    log_total = jnp.log(row_total)
    gap = maxima[1] - row_max[1][None] - log_total[1][None]
    cross_term = jnp.sum(lift[0] * (stats[1, :, 2] + gap * stats[1, :, 3]), axis=0) / row_total[0]

    token_index = lax.axis_index("mp") * row_share + lax.iota(jnp.int32, row_share)
    slab_index = token_index // slab_length
    position = token_index - slab_index * slab_length
    matches = slab_index[:, None] == lax.iota(jnp.int32, lengths.shape[0])[None, :]
    valid_len = jnp.sum(jnp.where(matches, lengths[None, :], 0), axis=1)
    valid_mask = (position < valid_len).astype(jnp.float32)
    valid_total = jnp.sum(lengths).astype(jnp.float32)
    token_loss = -valid_mask * cross_term
    here = lax.axis_index("dp")
    own_lift = lax.dynamic_index_in_dim(lift, here, axis=1, keepdims=False)
    factor = own_lift / row_total * (valid_mask / valid_total)[None]
    own_factor = jnp.where(is_target, factor[0], factor[1])
    other_factor = jnp.where(is_target, jnp.zeros_like(factor[0]), factor[0])
    weighted = (raised * own_factor[:, None] - incoming * other_factor[:, None]).astype(jnp.bfloat16)
    all_weighted = lax.all_gather(weighted, "mp", axis=0, tiled=True)
    summed = jnp.einsum(
        "tv,td->vd", all_weighted, draft_rows, preferred_element_type=jnp.float32
    )
    sign_factor = jnp.where(is_target, -1.0, 1.0).astype(jnp.float32)
    grad_terms = (sign_factor * summed).astype(jnp.bfloat16)[None]
    return (grad_terms, token_loss)


def solution(mesh):
    in_specs = (
        P(None, "mp", ("grp", "dp")),
        P(None, ("grp", "dp"), "mp"),
        P("grp", "dp", "mp"),
        P("dp", "mp"),
        P("mp"),
        P("mp"),
        P(),
    )
    out_specs = (P("grp", "dp", "mp"), P("mp"))
    return jax.shard_map(
        per_device, mesh=mesh, in_specs=in_specs, out_specs=out_specs, check_vma=False
    )
```

```python
import functools

import jax
import jax.numpy as jnp
from jax import lax
from jax.experimental import pallas as pl
from jax.experimental.pallas import tpu as pltpu
from jax.sharding import PartitionSpec as P

EPSILON = 1e-05
PARTIAL = jnp.bfloat16
MESH = pl.DeviceIdType.MESH


def whole_axis(axis):
    return lambda: (lax.axis_size(axis), lax.axis_index(axis), lambda p: {axis: p})


def both_axes():
    outer, inner = lax.axis_size("grp"), lax.axis_size("dp")
    me = lax.axis_index("grp") * inner + lax.axis_index("dp")
    return (outer * inner, me, lambda p: {"grp": lax.div(p, inner), "dp": lax.rem(p, inner)})


def pair():
    index = lax.axis_index("mp")
    return (2, lax.rem(index, 2), lambda p: {"mp": lax.div(index, 2) * 2 + p})


def across():
    index = lax.axis_index("mp")
    count = lax.axis_size("mp") // 2
    return (count, lax.div(index, 2), lambda p: {"mp": p * 2 + lax.rem(index, 2)})


def window(ref, dim, index, size):
    start = index * size if isinstance(index, int) else pl.multiple_of(index * size, size)
    return ref.at[(slice(None),) * dim + (pl.ds(start, size),)]


def exchange_body(items, *refs):
    count = len(items)
    ins, outs = refs[:count], refs[count : 2 * count]
    local_sem, send_sem, recv_sem = refs[2 * count :]
    groups = [item[0]() for item in items]
    barrier = pltpu.get_barrier_semaphore()
    total = 0
    for n, me, place in groups:
        for k in range(1, n):
            pl.semaphore_signal(
                barrier, inc=1, device_id=place(lax.rem(me + k, n)), device_id_type=MESH
            )
        total += n - 1
    pl.semaphore_wait(barrier, total)
    copies = []
    slot = 0
    for number, ((_, kind, dim, cut, pieces), (n, me, place)) in enumerate(zip(items, groups)):
        source, target = ins[number], outs[number]
        step = source.shape[cut] // pieces
        for k in range(1, n):
            peer = lax.rem(me + k, n)
            if kind == "gather":
                sent, landing = source, window(target, dim, me, source.shape[dim])
            else:
                size = source.shape[dim] // n
                sent, landing = window(source, dim, peer, size), window(target, dim, k - 1, size)
            for piece in range(pieces):
                copy = pltpu.make_async_remote_copy(
                    src_ref=sent if pieces == 1 else window(sent, cut, piece, step),
                    dst_ref=landing if pieces == 1 else window(landing, cut, piece, step),
                    send_sem=send_sem.at[slot],
                    recv_sem=recv_sem.at[slot],
                    device_id=place(peer),
                    device_id_type=MESH,
                )
                copy.start()
                copies.append(copy)
                slot += 1
        if kind == "gather":
            own = pltpu.make_async_copy(
                source, window(target, dim, me, source.shape[dim]), local_sem.at[number]
            )
            own.start()
            copies.append(own)
    for copy in copies:
        copy.wait()


def exchange(number, arrays, items):
    shapes = []
    slots = 0
    for array, (group, kind, dim, cut, pieces) in zip(arrays, items):
        n = group()[0]
        slots += (n - 1) * pieces
        shape = list(array.shape)
        shape[dim] = shape[dim] * n if kind == "gather" else shape[dim] // n * (n - 1)
        shapes.append(jax.ShapeDtypeStruct(tuple(shape), array.dtype))
    return pl.pallas_call(
        functools.partial(exchange_body, items),
        out_shape=shapes,
        in_specs=[pl.BlockSpec(memory_space=pl.ANY)] * len(arrays),
        out_specs=[pl.BlockSpec(memory_space=pl.ANY)] * len(arrays),
        scratch_shapes=[
            pltpu.SemaphoreType.DMA((len(arrays),)),
            pltpu.SemaphoreType.DMA((slots,)),
            pltpu.SemaphoreType.DMA((slots,)),
        ],
        compiler_params=pltpu.CompilerParams(collective_id=number, has_side_effects=True),
    )(*arrays)


def summed_over(number, parts, group, pieces):
    (arrived,) = exchange(number, (parts,), ((group, "swap", 0, 1, pieces),))
    own = lax.dynamic_index_in_dim(parts, group()[1], axis=0, keepdims=False)
    total = own.astype(jnp.float32)
    for k in range(arrived.shape[0]):
        total = total + arrived[k].astype(jnp.float32)
    return total


def gathered_in_chip(numbers, array, cut, pieces):
    lifted = array[:, None, None]
    (lifted,) = exchange(numbers[0], (lifted,), ((across, "gather", 1, cut, pieces),))
    (lifted,) = exchange(numbers[1], (lifted,), ((pair, "gather", 2, cut, pieces),))
    return lifted.reshape(array.shape[0], -1, array.shape[2])


def unite_body(captured_ref, weight_ref, out_ref, total):
    layer = pl.program_id(1)

    @pl.when(layer == 0)
    def _():
        total[...] = jnp.zeros_like(total)

    total[...] += jnp.dot(captured_ref[0], weight_ref[0], preferred_element_type=jnp.float32)

    @pl.when(layer == pl.num_programs(1) - 1)
    def _():
        out_ref[...] = total[...].astype(out_ref.dtype)


def unite(segment, weight, tile=512):
    layers, tokens, depth = segment.shape
    columns = weight.shape[2]
    tile = min(tile, columns)
    return pl.pallas_call(
        unite_body,
        out_shape=jax.ShapeDtypeStruct((tokens, columns), PARTIAL),
        grid=(columns // tile, layers),
        in_specs=[
            pl.BlockSpec((1, tokens, depth), lambda c, l: (l, 0, 0)),
            pl.BlockSpec((1, depth, tile), lambda c, l: (l, 0, c)),
        ],
        out_specs=pl.BlockSpec((tokens, tile), lambda c, l: (0, c)),
        scratch_shapes=[pltpu.VMEM((tokens, tile), jnp.float32)],
        compiler_params=pltpu.CompilerParams(vmem_limit_bytes=32 * 2**20),
    )(segment, weight)


def logits_body(rows_ref, head_ref, out_ref):
    out_ref[...] = lax.dot_general(
        rows_ref[...], head_ref[0], (((1,), (1,)), ((), ())), preferred_element_type=jnp.float32
    )


def logits_of(rows, head, width, tile=512):
    tokens, depth = rows.shape
    tile = min(tile, width)
    return pl.pallas_call(
        logits_body,
        out_shape=jax.ShapeDtypeStruct((tokens, width), jnp.float32),
        grid=(pl.cdiv(width, tile),),
        in_specs=[
            pl.BlockSpec((tokens, depth), lambda v: (0, 0)),
            pl.BlockSpec((1, tile, depth), lambda v: (0, v, 0)),
        ],
        out_specs=pl.BlockSpec((tokens, tile), lambda v: (0, v)),
        compiler_params=pltpu.CompilerParams(vmem_limit_bytes=32 * 2**20),
    )(rows, head)


def as_tile(parts):
    flat = jnp.concatenate([part.reshape(-1) for part in parts])
    padded = -(-flat.shape[0] // 1024) * 1024
    return jnp.pad(flat, (0, padded - flat.shape[0])).reshape(1, -1, 128)


def per_device(captured, unite_weight, heads, final_hidden, target_gain, draft_gain, lengths):
    mp_size = lax.axis_size("mp")
    dp_size = lax.axis_size("dp")
    grp_size = lax.axis_size("grp")
    model_width = final_hidden.shape[1] * mp_size
    slab_length = final_hidden.shape[0]
    is_target = lax.axis_index("grp") == 0
    last = lax.all_gather(final_hidden, "dp", axis=0, tiled=True)
    segment = gathered_in_chip((1, 9), captured, 0, captured.shape[0])
    tokens = last.shape[0]
    running = unite(segment, unite_weight)
    members = grp_size * dp_size
    share = tokens // members
    united = summed_over(2, running.reshape(members, share, -1), both_axes, 1)
    last_values = last.astype(jnp.float32)
    (squares,) = exchange(
        3,
        (as_tile([jnp.sum(united * united, axis=1), jnp.sum(last_values * last_values, axis=1)]),),
        ((whole_axis("mp"), "gather", 0, 1, 1),),
    )
    squares = jnp.sum(squares, axis=0).reshape(-1)
    draft_scale = lax.rsqrt(squares[:share] / model_width + EPSILON)
    target_scale = lax.rsqrt(squares[share : share + tokens] / model_width + EPSILON)
    draft_part = (united * draft_scale[:, None] * draft_gain[None, :]).astype(jnp.bfloat16)
    target_rows = (last_values * target_scale[:, None] * target_gain[None, :]).astype(jnp.bfloat16)
    (draft_rows,) = exchange(4, (draft_part,), ((both_axes, "gather", 0, 1, 1),))
    own_rows = jnp.where(is_target, target_rows, draft_rows)
    row_share = tokens // mp_size
    vocab = heads.shape[1]
    width = -(-vocab // 128) * 128
    partial_logits = logits_of(own_rows, heads, width)
    by_core = partial_logits.reshape(mp_size // 2, 2, row_share, width)
    pieces = row_share // 8
    (swapped,) = exchange(5, (by_core,), ((pair, "swap", 1, 2, pieces),))
    by_chip = swapped[:, 0] + lax.dynamic_index_in_dim(by_core, pair()[1], axis=1, keepdims=False)
    logits = summed_over(6, by_chip, across, pieces)
    logits = jnp.where(lax.broadcasted_iota(jnp.int32, logits.shape, 1) < vocab, logits, -1e30)
    local_max = jnp.max(logits, axis=1)
    shifted = logits - local_max[:, None]
    raised = jnp.exp(shifted)
    local_total = jnp.sum(raised, axis=1)
    incoming = lax.ppermute(raised.astype(jnp.bfloat16), "grp", [(0, 1)]).astype(jnp.float32)
    crossed = jnp.sum(incoming * shifted, axis=1)
    incoming_total = jnp.sum(incoming, axis=1)
    (stats,) = exchange(
        7,
        (as_tile([local_max, local_total, crossed, incoming_total]),),
        ((both_axes, "gather", 0, 1, 1),),
    )
    stats = stats.reshape(grp_size, dp_size, -1)[:, :, : 4 * row_share]
    stats = stats.reshape(grp_size, dp_size, 4, row_share)
    maxima, totals = stats[:, :, 0], stats[:, :, 1]
    row_max = jnp.max(maxima, axis=1)
    lift = jnp.exp(maxima - row_max[:, None])
    row_total = jnp.sum(lift * totals, axis=1)
    log_total = jnp.log(row_total)
    gap = maxima[1] - row_max[1][None] - log_total[1][None]
    cross_term = jnp.sum(lift[0] * (stats[1, :, 2] + gap * stats[1, :, 3]), axis=0) / row_total[0]

    token_index = lax.axis_index("mp") * row_share + lax.iota(jnp.int32, row_share)
    slab_index = token_index // slab_length
    position = token_index - slab_index * slab_length
    matches = slab_index[:, None] == lax.iota(jnp.int32, lengths.shape[0])[None, :]
    valid_len = jnp.sum(jnp.where(matches, lengths[None, :], 0), axis=1)
    valid_mask = (position < valid_len).astype(jnp.float32)
    valid_total = jnp.sum(lengths).astype(jnp.float32)
    token_loss = -valid_mask * cross_term
    here = lax.axis_index("dp")
    own_lift = lax.dynamic_index_in_dim(lift, here, axis=1, keepdims=False)
    factor = own_lift / row_total * (valid_mask / valid_total)[None]
    own_factor = jnp.where(is_target, factor[0], factor[1])
    other_factor = jnp.where(is_target, jnp.zeros_like(factor[0]), factor[0])
    weighted = (raised * own_factor[:, None] - incoming * other_factor[:, None]).astype(jnp.bfloat16)
    all_weighted = gathered_in_chip((8, 10), weighted[None], 3, width // 1024 or 1)[0, :, :vocab]
    summed = jnp.einsum(
        "tv,td->vd", all_weighted, draft_rows, preferred_element_type=jnp.float32
    )
    sign_factor = jnp.where(is_target, -1.0, 1.0).astype(jnp.float32)
    grad_terms = (sign_factor * summed).astype(jnp.bfloat16)[None]
    return (grad_terms, token_loss)


def solution(mesh):
    in_specs = (
        P(None, "mp", ("grp", "dp")),
        P(None, ("grp", "dp"), "mp"),
        P("grp", "dp", "mp"),
        P("dp", "mp"),
        P("mp"),
        P("mp"),
        P(),
    )
    out_specs = (P("grp", "dp", "mp"), P("mp"))
    return jax.shard_map(
        per_device, mesh=mesh, in_specs=in_specs, out_specs=out_specs, check_vma=False
    )
```

```python
import functools

import jax
import jax.numpy as jnp
from jax import lax
from jax.experimental import pallas as pl
from jax.experimental.pallas import tpu as pltpu
from jax.sharding import PartitionSpec as P

EPSILON = 1e-05
PARTIAL = jnp.bfloat16
MESH = pl.DeviceIdType.MESH


def whole_axis(axis):
    return lambda: (lax.axis_size(axis), lax.axis_index(axis), lambda p: {axis: p})


def both_axes():
    outer, inner = lax.axis_size("grp"), lax.axis_size("dp")
    me = lax.axis_index("grp") * inner + lax.axis_index("dp")
    return (outer * inner, me, lambda p: {"grp": lax.div(p, inner), "dp": lax.rem(p, inner)})


def pair():
    index = lax.axis_index("mp")
    return (2, lax.rem(index, 2), lambda p: {"mp": lax.div(index, 2) * 2 + p})


def across():
    index = lax.axis_index("mp")
    count = lax.axis_size("mp") // 2
    return (count, lax.div(index, 2), lambda p: {"mp": p * 2 + lax.rem(index, 2)})


def window(ref, dim, index, size):
    start = index * size if isinstance(index, int) else pl.multiple_of(index * size, size)
    return ref.at[(slice(None),) * dim + (pl.ds(start, size),)]


def exchange_body(items, *refs):
    count = len(items)
    ins, outs = refs[:count], refs[count : 2 * count]
    local_sem, send_sem, recv_sem = refs[2 * count : 2 * count + 3]
    held = refs[2 * count + 3 :]
    groups = [item[0]() for item in items]
    barrier = pltpu.get_barrier_semaphore()
    total = 0
    for n, me, place in groups:
        for k in range(1, n):
            pl.semaphore_signal(
                barrier, inc=1, device_id=place(lax.rem(me + k, n)), device_id_type=MESH
            )
        total += n - 1
    pl.semaphore_wait(barrier, total)
    copies = []
    slot = 0
    for number, ((_, kind, dim, cut, pieces), (n, me, place)) in enumerate(zip(items, groups)):
        source, target = ins[number], outs[number]
        step = source.shape[cut] // pieces
        for k in range(1, n):
            peer = lax.rem(me + k, n)
            if kind == "gather":
                sent, landing = source, window(target, dim, me, source.shape[dim])
            else:
                size = source.shape[dim] // n
                sent, landing = window(source, dim, peer, size), window(target, dim, k - 1, size)
            for piece in range(pieces):
                copy = pltpu.make_async_remote_copy(
                    src_ref=sent if pieces == 1 else window(sent, cut, piece, step),
                    dst_ref=landing if pieces == 1 else window(landing, cut, piece, step),
                    send_sem=send_sem.at[slot],
                    recv_sem=recv_sem.at[slot],
                    device_id=place(peer),
                    device_id_type=MESH,
                )
                copy.start()
                copies.append(copy)
                slot += 1
        if kind == "gather":
            taken = pltpu.make_async_copy(source, held[number], local_sem.at[number])
            taken.start()
            taken.wait()
            own = pltpu.make_async_copy(
                held[number], window(target, dim, me, source.shape[dim]), local_sem.at[number]
            )
            own.start()
            copies.append(own)
    for copy in copies:
        copy.wait()


def exchange(number, arrays, items):
    shapes = []
    slots = 0
    for array, (group, kind, dim, cut, pieces) in zip(arrays, items):
        n = group()[0]
        slots += (n - 1) * pieces
        shape = list(array.shape)
        shape[dim] = shape[dim] * n if kind == "gather" else shape[dim] // n * (n - 1)
        shapes.append(jax.ShapeDtypeStruct(tuple(shape), array.dtype))
    return pl.pallas_call(
        functools.partial(exchange_body, items),
        out_shape=shapes,
        in_specs=[pl.BlockSpec(memory_space=pl.ANY)] * len(arrays),
        out_specs=[pl.BlockSpec(memory_space=pl.ANY)] * len(arrays),
        scratch_shapes=[
            pltpu.SemaphoreType.DMA((len(arrays),)),
            pltpu.SemaphoreType.DMA((slots,)),
            pltpu.SemaphoreType.DMA((slots,)),
        ]
        + [
            pltpu.VMEM(array.shape if item[1] == "gather" else (8, 128), array.dtype)
            for array, item in zip(arrays, items)
        ],
        compiler_params=pltpu.CompilerParams(collective_id=number, has_side_effects=True),
    )(*arrays)


def summed_over(number, parts, group, pieces):
    (arrived,) = exchange(number, (parts,), ((group, "swap", 0, 1, pieces),))
    own = lax.dynamic_index_in_dim(parts, group()[1], axis=0, keepdims=False)
    total = own.astype(jnp.float32)
    for k in range(arrived.shape[0]):
        total = total + arrived[k].astype(jnp.float32)
    return total


def gathered_in_chip(numbers, array, cut, pieces):
    lifted = array[:, None, None]
    (lifted,) = exchange(numbers[0], (lifted,), ((across, "gather", 1, cut, pieces),))
    (lifted,) = exchange(numbers[1], (lifted,), ((pair, "gather", 2, cut, pieces),))
    return lifted.reshape(array.shape[0], -1, array.shape[2])


def unite_body(captured_ref, weight_ref, out_ref, total):
    layer = pl.program_id(1)

    @pl.when(layer == 0)
    def _():
        total[...] = jnp.zeros_like(total)

    total[...] += jnp.dot(captured_ref[0], weight_ref[0], preferred_element_type=jnp.float32)

    @pl.when(layer == pl.num_programs(1) - 1)
    def _():
        out_ref[...] = total[...].astype(out_ref.dtype)


def unite(segment, weight, tile=512):
    layers, tokens, depth = segment.shape
    columns = weight.shape[2]
    tile = min(tile, columns)
    return pl.pallas_call(
        unite_body,
        out_shape=jax.ShapeDtypeStruct((tokens, columns), PARTIAL),
        grid=(columns // tile, layers),
        in_specs=[
            pl.BlockSpec((1, tokens, depth), lambda c, l: (l, 0, 0)),
            pl.BlockSpec((1, depth, tile), lambda c, l: (l, 0, c)),
        ],
        out_specs=pl.BlockSpec((tokens, tile), lambda c, l: (0, c)),
        scratch_shapes=[pltpu.VMEM((tokens, tile), jnp.float32)],
        compiler_params=pltpu.CompilerParams(vmem_limit_bytes=32 * 2**20),
    )(segment, weight)


def logits_body(rows_ref, head_ref, out_ref):
    out_ref[...] = lax.dot_general(
        rows_ref[...], head_ref[0], (((1,), (1,)), ((), ())), preferred_element_type=jnp.float32
    )


def logits_of(rows, head, width, tile=512):
    tokens, depth = rows.shape
    tile = min(tile, width)
    return pl.pallas_call(
        logits_body,
        out_shape=jax.ShapeDtypeStruct((tokens, width), jnp.float32),
        grid=(pl.cdiv(width, tile),),
        in_specs=[
            pl.BlockSpec((tokens, depth), lambda v: (0, 0)),
            pl.BlockSpec((1, tile, depth), lambda v: (0, v, 0)),
        ],
        out_specs=pl.BlockSpec((tokens, tile), lambda v: (0, v)),
        compiler_params=pltpu.CompilerParams(vmem_limit_bytes=32 * 2**20),
    )(rows, head)


def as_tile(parts):
    flat = jnp.concatenate([part.reshape(-1) for part in parts])
    padded = -(-flat.shape[0] // 1024) * 1024
    return jnp.pad(flat, (0, padded - flat.shape[0])).reshape(1, -1, 128)


def per_device(captured, unite_weight, heads, final_hidden, target_gain, draft_gain, lengths):
    mp_size = lax.axis_size("mp")
    dp_size = lax.axis_size("dp")
    grp_size = lax.axis_size("grp")
    model_width = final_hidden.shape[1] * mp_size
    slab_length = final_hidden.shape[0]
    is_target = lax.axis_index("grp") == 0
    last = lax.all_gather(final_hidden, "dp", axis=0, tiled=True)
    segment = gathered_in_chip((1, 9), captured, 0, captured.shape[0])
    tokens = last.shape[0]
    running = unite(segment, unite_weight)
    members = grp_size * dp_size
    share = tokens // members
    united = summed_over(2, running.reshape(members, share, -1), both_axes, 1)
    last_values = last.astype(jnp.float32)
    (squares,) = exchange(
        3,
        (as_tile([jnp.sum(united * united, axis=1), jnp.sum(last_values * last_values, axis=1)]),),
        ((whole_axis("mp"), "gather", 0, 1, 1),),
    )
    squares = jnp.sum(squares, axis=0).reshape(-1)
    draft_scale = lax.rsqrt(squares[:share] / model_width + EPSILON)
    target_scale = lax.rsqrt(squares[share : share + tokens] / model_width + EPSILON)
    draft_part = (united * draft_scale[:, None] * draft_gain[None, :]).astype(jnp.bfloat16)
    target_rows = (last_values * target_scale[:, None] * target_gain[None, :]).astype(jnp.bfloat16)
    (draft_rows,) = exchange(4, (draft_part,), ((both_axes, "gather", 0, 1, 1),))
    own_rows = jnp.where(is_target, target_rows, draft_rows)
    row_share = tokens // mp_size
    vocab = heads.shape[1]
    width = -(-vocab // 128) * 128
    partial_logits = logits_of(own_rows, heads, width)
    by_core = partial_logits.reshape(mp_size // 2, 2, row_share, width)
    pieces = row_share // 8
    (swapped,) = exchange(5, (by_core,), ((pair, "swap", 1, 2, pieces),))
    by_chip = swapped[:, 0] + lax.dynamic_index_in_dim(by_core, pair()[1], axis=1, keepdims=False)
    logits = summed_over(6, by_chip, across, pieces)
    logits = jnp.where(lax.broadcasted_iota(jnp.int32, logits.shape, 1) < vocab, logits, -1e30)
    local_max = jnp.max(logits, axis=1)
    shifted = logits - local_max[:, None]
    raised = jnp.exp(shifted)
    local_total = jnp.sum(raised, axis=1)
    incoming = lax.ppermute(raised.astype(jnp.bfloat16), "grp", [(0, 1)]).astype(jnp.float32)
    crossed = jnp.sum(incoming * shifted, axis=1)
    incoming_total = jnp.sum(incoming, axis=1)
    (stats,) = exchange(
        7,
        (as_tile([local_max, local_total, crossed, incoming_total]),),
        ((both_axes, "gather", 0, 1, 1),),
    )
    stats = stats.reshape(grp_size, dp_size, -1)[:, :, : 4 * row_share]
    stats = stats.reshape(grp_size, dp_size, 4, row_share)
    maxima, totals = stats[:, :, 0], stats[:, :, 1]
    row_max = jnp.max(maxima, axis=1)
    lift = jnp.exp(maxima - row_max[:, None])
    row_total = jnp.sum(lift * totals, axis=1)
    log_total = jnp.log(row_total)
    gap = maxima[1] - row_max[1][None] - log_total[1][None]
    cross_term = jnp.sum(lift[0] * (stats[1, :, 2] + gap * stats[1, :, 3]), axis=0) / row_total[0]

    token_index = lax.axis_index("mp") * row_share + lax.iota(jnp.int32, row_share)
    slab_index = token_index // slab_length
    position = token_index - slab_index * slab_length
    matches = slab_index[:, None] == lax.iota(jnp.int32, lengths.shape[0])[None, :]
    valid_len = jnp.sum(jnp.where(matches, lengths[None, :], 0), axis=1)
    valid_mask = (position < valid_len).astype(jnp.float32)
    valid_total = jnp.sum(lengths).astype(jnp.float32)
    token_loss = -valid_mask * cross_term
    here = lax.axis_index("dp")
    own_lift = lax.dynamic_index_in_dim(lift, here, axis=1, keepdims=False)
    factor = own_lift / row_total * (valid_mask / valid_total)[None]
    own_factor = jnp.where(is_target, factor[0], factor[1])
    other_factor = jnp.where(is_target, jnp.zeros_like(factor[0]), factor[0])
    weighted = (raised * own_factor[:, None] - incoming * other_factor[:, None]).astype(jnp.bfloat16)
    all_weighted = gathered_in_chip((8, 10), weighted[None], 3, width // 1024 or 1)[0, :, :vocab]
    summed = jnp.einsum(
        "tv,td->vd", all_weighted, draft_rows, preferred_element_type=jnp.float32
    )
    sign_factor = jnp.where(is_target, -1.0, 1.0).astype(jnp.float32)
    grad_terms = (sign_factor * summed).astype(jnp.bfloat16)[None]
    return (grad_terms, token_loss)


def solution(mesh):
    in_specs = (
        P(None, "mp", ("grp", "dp")),
        P(None, ("grp", "dp"), "mp"),
        P("grp", "dp", "mp"),
        P("dp", "mp"),
        P("mp"),
        P("mp"),
        P(),
    )
    out_specs = (P("grp", "dp", "mp"), P("mp"))
    return jax.shard_map(
        per_device, mesh=mesh, in_specs=in_specs, out_specs=out_specs, check_vma=False
    )
```
